32 devices in a mesh: groups: 2 (over x), horiz: 16 (over z, y, core).
Axes of the slice: x: 2, y: 2, z: 4, core: 2. Of those that a mesh axis runs over, the one named last changes fastest.
Arguments:
- leaf_nodes: float32 [128, 16, 3072], P('groups', 'horiz'), parts along dimension 0, may hold values from -6 to 6
- compress: float32 [32, 64], replicated, may hold values from -0.75 to 0.75
- expand: float32 [64, 32], replicated, may hold values from -1 to 1
- transfer: float32 [64, 512], replicated, may hold values from -0.25 to 0.25
- m2l_table: float32 [316, 1024], replicated, may hold values from -0.078125 to 0.078125
Outputs:
- leaf_local: float32 [128, 16, 3072], P('groups', 'horiz'), parts along dimension 0
The draws below stay inside these ranges and needn't reach their ends.
There are 2 independent parts, one for each index of `groups`. The reference program is written for one: setup_inputs(seed, part) draws one part's arguments, and reference() takes and returns one part's arrays. A program takes and returns all parts, laid end to end along the dimension named above; an argument that names none is the same for every part. Nothing has to cross between parts.
All inputs are finite; a program needn't handle non-finite values.
Results may differ from the reference program's by a relative error of at most 0.0001.
Values sent between devices are 32-bit elements; how exact they have to be, the bound alone decides.
A program may use at most 128 MiB of HBM per device.

```python
import jax
import jax.numpy as jnp
from jax import lax

NODES = 64
RANK = 32
VECS = 316
GRID_X = 8
PX_DEV = 4
PY_DEV = 4
PZ = 24
TILES = 16
LEAF_DEV = 3072


def level_of(stream_key, shape, cuts, smallest, top_value):
    factor_of, own = 1.0, jax.random.fold_in(stream_key, 6)
    for position, parts in cuts:
        steps = jnp.exp(jax.random.uniform(jax.random.fold_in(own, position), (parts,), jnp.float32, smallest / len(cuts), top_value / len(cuts)))
        factor_of = factor_of * jnp.repeat(steps, shape[position] // parts).reshape([-1 if axis == position else 1 for axis in range(len(shape))])
    return factor_of


def centred(stream_key, shape, spread, limit, shards=(), kind=jnp.bfloat16):
    gain = level_of(stream_key, shape, shards, -0.22, 0.18) if shards else 1.0
    values = jax.random.normal(stream_key, shape, jnp.float32) * spread * gain
    return jnp.minimum(jnp.maximum(values, -limit), limit).astype(kind)


def setup_inputs(seed: int = 0, part: int = 0) -> dict:
    seeds = jax.random.split(jax.random.key(seed), 6)
    own_keys = jax.random.split(jax.random.fold_in(seeds[5], part), 6)
    return {
        "leaf_nodes": centred(own_keys[0], (NODES, TILES, LEAF_DEV), 1.0, 6.0, ((1, 16),), jnp.float32),
        "compress": centred(seeds[1], (RANK, NODES), NODES ** -0.5, 0.75, (), jnp.float32),
        "expand": centred(seeds[2], (NODES, RANK), RANK ** -0.5, 1.0, (), jnp.float32),
        "transfer": centred(seeds[3], (NODES, 8 * NODES), (8 * NODES) ** -0.5, 0.25, (), jnp.float32),
        "m2l_table": centred(seeds[4], (VECS, RANK * RANK), (189 * RANK) ** -0.5, 0.078125, (), jnp.float32),
    }


HIGHEST = lax.Precision.HIGHEST
OFFSETS = [(shift_x, shift_y, shift_z) for shift_x in (-1, 0, 1) for shift_y in (-1, 0, 1) for shift_z in (-1, 0, 1)]


def full_table(m2l_table, rank_count):
    pieces = []
    start_at = 0
    zeros_three = jnp.zeros((3, m2l_table.shape[1]), jnp.float32)
    for step_a in range(-3, 4):
        for step_b in range(-3, 4):
            if max(abs(step_a), abs(step_b)) >= 2:
                pieces.append(m2l_table[start_at:start_at + 7])
                start_at = start_at + 7
            else:
                pieces.append(m2l_table[start_at:start_at + 2])
                pieces.append(zeros_three)
                pieces.append(m2l_table[start_at + 2:start_at + 4])
                start_at = start_at + 4
    return jnp.concatenate(pieces, axis=0).reshape(7, 7, 7, rank_count, rank_count)


def m2l_blocks(m2l_table, rank_count):
    table_cube = full_table(m2l_table, rank_count)
    blocks = []
    for shift_x, shift_y, shift_z in OFFSETS:
        targets = []
        for target in range(8):
            lower_x = 2 * shift_x + 3 - (target >> 2)
            lower_y = 2 * shift_y + 3 - ((target >> 1) & 1)
            lower_z = 2 * shift_z + 3 - (target & 1)
            window = table_cube[lower_x:lower_x + 2, lower_y:lower_y + 2, lower_z:lower_z + 2]
            targets.append(window.reshape(8, rank_count, rank_count))
        stacked = jnp.stack(targets)
        blocks.append(stacked.transpose(1, 3, 0, 2).reshape(8 * rank_count, 8 * rank_count))
    return jnp.stack(blocks)


def compress_leaves(compress, leaf_grid):
    extent_x, extent_y, extent_z = leaf_grid.shape[2:]
    charged = jnp.einsum("rn,ncxyz->xyzcr", compress, leaf_grid, precision=HIGHEST)
    return charged.reshape(extent_x, extent_y, extent_z, -1)


def coarse_charges(compress, transfer, leaf_grid):
    node_count = leaf_grid.shape[0]
    rank_count = compress.shape[0]
    extent_x, extent_y, extent_z = leaf_grid.shape[2:]
    coarse_nodes = jnp.einsum("nkm,mkxyz->nxyz", transfer.reshape(node_count, 8, node_count), leaf_grid, precision=HIGHEST)
    charged = jnp.einsum("rn,nxyz->xyzr", compress, coarse_nodes, precision=HIGHEST)
    charged = charged.reshape(extent_x // 2, 2, extent_y // 2, 2, extent_z // 2, 2, rank_count)
    return charged.transpose(0, 2, 4, 1, 3, 5, 6).reshape(extent_x // 2, extent_y // 2, extent_z // 2, -1)


def far_field(padded, blocks):
    extent_x = padded.shape[0] - 2
    extent_y = padded.shape[1] - 2
    extent_z = padded.shape[2] - 2
    channels = padded.shape[3]
    accumulated = jnp.zeros((extent_x * extent_y * extent_z, blocks.shape[2]), jnp.float32)
    for offset_id, (shift_x, shift_y, shift_z) in enumerate(OFFSETS):
        window = padded[1 + shift_x:1 + shift_x + extent_x, 1 + shift_y:1 + shift_y + extent_y, 1 + shift_z:1 + shift_z + extent_z]
        accumulated = accumulated + jnp.dot(window.reshape(-1, channels), blocks[offset_id], precision=HIGHEST)
    return accumulated.reshape(extent_x, extent_y, extent_z, -1)


def local_expansions(expand, transfer, fine_field, coarse_field):
    node_count, rank_count = expand.shape
    extent_x, extent_y, extent_z = fine_field.shape[:3]
    half_x, half_y, half_z = coarse_field.shape[:3]
    direct = jnp.einsum("nr,xyzcr->ncxyz", expand, fine_field.reshape(extent_x, extent_y, extent_z, 8, rank_count), precision=HIGHEST)
    coarse_local = jnp.einsum("nr,xyzcr->nxyzc", expand, coarse_field.reshape(half_x, half_y, half_z, 8, rank_count), precision=HIGHEST)
    coarse_local = coarse_local.reshape(node_count, half_x, half_y, half_z, 2, 2, 2).transpose(0, 1, 4, 2, 5, 3, 6)
    coarse_local = coarse_local.reshape(node_count, extent_x, extent_y, extent_z)
    pushed = jnp.einsum("mkn,mxyz->nkxyz", transfer.reshape(node_count, 8, node_count), coarse_local, precision=HIGHEST)
    return direct + pushed


def reference(leaf_nodes, compress, expand, transfer, m2l_table):
    node_count = leaf_nodes.shape[0]
    rank_count = compress.shape[0]
    grid_rows = leaf_nodes.shape[1] // GRID_X
    whole_x = GRID_X * PX_DEV
    whole_y = grid_rows * PY_DEV
    tiled = leaf_nodes.reshape(node_count, GRID_X, grid_rows, 8, PX_DEV, PY_DEV, PZ)
    leaf_grid = tiled.transpose(0, 3, 1, 4, 2, 5, 6).reshape(node_count, 8, whole_x, whole_y, PZ)
    fine_charge = compress_leaves(compress, leaf_grid)
    coarse_charge = coarse_charges(compress, transfer, leaf_grid)
    padding = ((1, 1), (1, 1), (1, 1), (0, 0))
    blocks = m2l_blocks(m2l_table, rank_count)
    fine_field = far_field(jnp.pad(fine_charge, padding), blocks)
    coarse_field = 0.5 * far_field(jnp.pad(coarse_charge, padding), blocks)
    result = local_expansions(expand, transfer, fine_field, coarse_field)
    result = result.reshape(node_count, 8, GRID_X, PX_DEV, grid_rows, PY_DEV, PZ).transpose(0, 2, 4, 1, 3, 5, 6)
    return result.reshape(node_count, GRID_X * grid_rows, -1)
```

```python
import functools

import jax
import jax.numpy as jnp
import ml_dtypes
import numpy as np
from jax import lax
from jax.experimental import pallas as pl
from jax.experimental.pallas import tpu as pltpu
from jax.sharding import PartitionSpec as P

GRID_X = 8
PX = 4
PY = 4
PZ = 24
BOXES = PX * PY * PZ
COARSE_Z = 16
COARSE_ROWS = (PX // 2) * (PY // 2) * COARSE_Z
HIGHEST = lax.Precision.HIGHEST
BF16 = jnp.bfloat16
F32 = jnp.float32
DIRECTIONS = [(0, -1), (0, 1), (-1, 0), (1, 0), (-1, -1), (-1, 1), (1, -1), (1, 1)]
RIM_ROWS = PX * PZ + (PX // 2) * COARSE_Z
NT = (((1,), (1,)), ((), ()))


def table_selection():
    select = np.zeros((8 * 56, 316), np.float32)
    row = 0
    for dx in range(7):
        for dy in range(7):
            for dz in range(7):
                if max(abs(dx - 3), abs(dy - 3), abs(dz - 3)) >= 2:
                    select[dz * 56 + dx * 7 + dy, row] = 1.0
                    row += 1
    return select.astype(ml_dtypes.bfloat16)


def parent_selection():
    select = np.zeros((8 * COARSE_ROWS, BOXES), np.float32)
    for bx in range(PX):
        for by in range(PY):
            for bz in range(PZ):
                child = 4 * (bx % 2) + 2 * (by % 2) + bz % 2
                parent = ((bx // 2) * (PY // 2) + by // 2) * COARSE_Z + bz // 2
                select[child * COARSE_ROWS + parent, (bx * PY + by) * PZ + bz] = 1.0
    return select.astype(ml_dtypes.bfloat16)


def split(value):
    high = value.astype(BF16)
    return high, (value - high.astype(F32)).astype(BF16)


def select_dot(value, select, dims):
    high, low = split(value)
    return lax.dot_general(high, select, dims, preferred_element_type=F32) + lax.dot_general(
        low, select, dims, preferred_element_type=F32
    )


def weights_kernel(table_ref, select_ref, high_ref, low_ref, cube, lanes_a, lanes_b):
    table_high, table_low = split(table_ref[...])
    select = select_ref[...]
    cube[...] = jnp.dot(select, table_high, preferred_element_type=F32) + jnp.dot(
        select, table_low, preferred_element_type=F32
    )
    slot = lax.broadcasted_iota(jnp.int32, (56, 128), 1) // 32
    for half, out in enumerate((lanes_a, lanes_b)):
        for tile in range(8):
            parts = [
                cube[(4 * half + k) * 56 : (4 * half + k + 1) * 56, tile * 128 : (tile + 1) * 128]
                for k in range(4)
            ]
            for inner in range(4):
                merged = None
                for k in range(4):
                    by = (k - inner) % 4 * 32
                    moved = pltpu.roll(parts[k], by, 1) if by else parts[k]
                    merged = moved if merged is None else jnp.where(slot == k, moved, merged)
                out[pl.ds(tile * 4 + inner, 56, stride=32), :] = merged
    low_half = lax.broadcasted_iota(jnp.int32, (192, 128), 1) < 64
    lane = lax.broadcasted_iota(jnp.int32, (224, 128), 1)
    for dx in range(7):
        even0 = lanes_a[dx * 224 : (dx + 1) * 224, :]
        even1 = lanes_b[dx * 224 : (dx + 1) * 224, :]
        turned0 = pltpu.roll(even0, 96, 1)
        turned1 = pltpu.roll(even1, 96, 1)
        odd0 = jnp.where(lane < 96, turned0, turned1)
        odd1 = turned1
        for w, (source, straight) in enumerate(
            ((even0, True), (odd0, True), (even0, False), (odd0, False), (even1, True), (odd1, True))
        ):
            other = pltpu.roll(source, 64, 1)
            first, second = (source, other) if straight else (other, source)
            high, low = split(jnp.where(low_half, first[:192], second[32:]))
            high_ref[w * 7 + dx] = high
            low_ref[w * 7 + dx] = low


def charges_kernel(
    grid_rows, leaf_ref, compress_ref, transfer_ref, select_ref, fine_ref, coarse_ref, halo_ref,
    rim, send_sem, recv_sem,
):
    here = lax.axis_index("horiz")
    tile_x = here // grid_rows
    tile_y = here % grid_rows

    def present(dx, dy):
        x, y = tile_x + dx, tile_y + dy
        return (x >= 0) & (x < GRID_X) & (y >= 0) & (y < grid_rows)

    barrier = pltpu.get_barrier_semaphore()
    for dx, dy in DIRECTIONS:
        @pl.when(present(dx, dy))
        def _(dx=dx, dy=dy):
            pl.semaphore_signal(
                barrier, inc=1, device_id={"horiz": here + dx * grid_rows + dy},
                device_id_type=pl.DeviceIdType.MESH,
            )

    compress = compress_ref[...]
    fine, nodes = [], None
    for child in range(8):
        leaf = leaf_ref[:, child * BOXES : (child + 1) * BOXES]
        fine.append(jnp.dot(compress, leaf, precision=HIGHEST, preferred_element_type=F32))
        term = jnp.dot(
            transfer_ref[:, child * 64 : (child + 1) * 64], leaf, precision=HIGHEST,
            preferred_element_type=F32,
        )
        nodes = term if nodes is None else nodes + term
    fine_ref[...] = jnp.concatenate(fine, axis=0).T
    coarse = jnp.dot(compress, nodes, precision=HIGHEST, preferred_element_type=F32)
    grouped = select_dot(coarse, select_ref[...], NT)
    coarse_ref[...] = jnp.concatenate(
        [grouped[:, c * COARSE_ROWS : (c + 1) * COARSE_ROWS] for c in range(8)], axis=0
    ).T

    def pick(step, extent):
        return range(extent) if step == 0 else ([extent - 1] if step > 0 else [0])

    lengths = []
    for number, (dx, dy) in enumerate(DIRECTIONS):
        at = 0
        for x in pick(dx, PX):
            for y in pick(dy, PY):
                start = (x * PY + y) * PZ
                rim[number, at : at + PZ, :] = fine_ref[start : start + PZ, :]
                at += PZ
        for x in pick(dx, PX // 2):
            for y in pick(dy, PY // 2):
                start = (x * (PY // 2) + y) * COARSE_Z
                rim[number, at : at + COARSE_Z, :] = coarse_ref[start : start + COARSE_Z, :]
                at += COARSE_Z
        lengths.append(at)

    peers = sum(jnp.where(present(dx, dy), 1, 0) for dx, dy in DIRECTIONS)
    pl.semaphore_wait(barrier, peers)

    def copy_of(number):
        dx, dy = DIRECTIONS[number]
        return pltpu.make_async_remote_copy(
            src_ref=rim.at[number, pl.ds(0, lengths[number])],
            dst_ref=halo_ref.at[number, pl.ds(0, lengths[number])],
            send_sem=send_sem.at[number],
            recv_sem=recv_sem.at[number],
            device_id={"horiz": here + dx * grid_rows + dy},
            device_id_type=pl.DeviceIdType.MESH,
        )

    for number, (dx, dy) in enumerate(DIRECTIONS):
        @pl.when(present(dx, dy))
        def _(number=number):
            copy_of(number).start()

    for number, (dx, dy) in enumerate(DIRECTIONS):
        @pl.when(jnp.logical_not(present(-dx, -dy)))
        def _(number=number):
            halo_ref[number] = jnp.zeros(halo_ref.shape[1:], F32)

    for number, (dx, dy) in enumerate(DIRECTIONS):
        @pl.when(present(dx, dy))
        def _(number=number):
            copy_of(number).wait_send()

        @pl.when(present(-dx, -dy))
        def _(number=number):
            copy_of(number).wait_recv()


def field_kernel(
    fine_ref, coarse_ref, halo_ref, high_ref, low_ref, expand_ref, transfer_ref, select_ref, out_ref,
    wide, wide_coarse, wins_high, wins_low, cwins_high, cwins_low, total,
):
    zero_rows = jnp.zeros((8, 256), F32)

    def place(x, y, rows):
        wide[x, y, 0:8, :] = zero_rows
        wide[x, y, 8 : 8 + PZ, :] = rows
        wide[x, y, 8 + PZ : 16 + PZ, :] = zero_rows

    def place_coarse(x, y, rows):
        wide_coarse[x, y, 0:8, :] = zero_rows
        wide_coarse[x, y, 8 : 8 + COARSE_Z, :] = rows
        wide_coarse[x, y, 8 + COARSE_Z : 16 + COARSE_Z, :] = zero_rows

    for x in range(PX):
        for y in range(PY):
            start = (x * PY + y) * PZ
            place(x + 1, y + 1, fine_ref[start : start + PZ, :])
    for x in range(PX // 2):
        for y in range(PY // 2):
            start = (x * (PY // 2) + y) * COARSE_Z
            place_coarse(x + 1, y + 1, coarse_ref[start : start + COARSE_Z, :])

    def rim_places(step, extent):
        return range(1, extent + 1) if step == 0 else ([0] if step > 0 else [extent + 1])

    for number, (dx, dy) in enumerate(DIRECTIONS):
        at = 0
        for x in rim_places(dx, PX):
            for y in rim_places(dy, PY):
                place(x, y, halo_ref[number, at : at + PZ, :])
                at += PZ
        for x in rim_places(dx, PX // 2):
            for y in rim_places(dy, PY // 2):
                place_coarse(x, y, halo_ref[number, at : at + COARSE_Z, :])
                at += COARSE_Z

    span = PY * PZ
    for sy in range(3):
        for sz in range(3):
            for x in range(PX + 2):
                rows = jnp.concatenate(
                    [wide[x, sy + y, 7 + sz : 7 + sz + PZ, :] for y in range(PY)], axis=0
                )
                high, low = split(rows)
                wins_high[sy, x * span : (x + 1) * span, sz * 256 : (sz + 1) * 256] = high
                wins_low[sy, x * span : (x + 1) * span, sz * 256 : (sz + 1) * 256] = low
            for sx in range(3):
                rows = jnp.concatenate(
                    [
                        wide_coarse[sx + x, sy + y, 7 + sz : 7 + sz + COARSE_Z, :]
                        for x in range(PX // 2)
                        for y in range(PY // 2)
                    ],
                    axis=0,
                )
                high, low = split(rows)
                cwins_high[sx * 3 + sy, :, sz * 256 : (sz + 1) * 256] = high
                cwins_low[sx * 3 + sy, :, sz * 256 : (sz + 1) * 256] = low

    total[...] = jnp.zeros_like(total)

    def weight(ref, sx, sy, sz):
        rows = []
        for target in range(8):
            tx, ty, tz = target >> 2, target >> 1 & 1, target & 1
            at_y = pl.multiple_of((2 * sy + 1 - ty) * 32, 32)
            first = (2 * sz + 1 - tz) * 7 + 2 * sx + 1 - tx
            rows.append(
                jnp.concatenate(
                    [ref[first, pl.ds(at_y, 32), :], ref[first + 1, pl.ds(at_y, 32), :]], axis=1
                )
            )
        return jnp.concatenate(rows, axis=0)

    def step(at, carry):
        sx, sy = at // 3, at % 3
        rows = pl.ds(pl.multiple_of(sx * span, 32), PX * span)
        high = jnp.concatenate([wins_high[sy, rows, :], cwins_high[at]], axis=0)
        low = jnp.concatenate([wins_low[sy, rows, :], cwins_low[at]], axis=0)
        by_high = jnp.concatenate([weight(high_ref, sx, sy, sz) for sz in range(3)], axis=1)
        by_low = jnp.concatenate([weight(low_ref, sx, sy, sz) for sz in range(3)], axis=1)
        total[...] += lax.dot_general(
            jnp.concatenate([high, low, high], axis=1),
            jnp.concatenate([by_high, by_high, by_low], axis=1),
            NT,
            preferred_element_type=F32,
        )
        return carry

    lax.fori_loop(0, 9, step, 0)

    expand = expand_ref[...]
    local = jnp.concatenate(
        [
            lax.dot_general(
                expand, 0.5 * total[BOXES:, c * 32 : (c + 1) * 32], NT, precision=HIGHEST,
                preferred_element_type=F32,
            )
            for c in range(8)
        ],
        axis=1,
    )
    coarse_local = select_dot(local, select_ref[...], (((1,), (0,)), ((), ())))
    for c in range(8):
        direct = lax.dot_general(
            expand, total[:BOXES, c * 32 : (c + 1) * 32], NT, precision=HIGHEST,
            preferred_element_type=F32,
        )
        pushed = lax.dot_general(
            transfer_ref[:, c * 64 : (c + 1) * 64], coarse_local, (((0,), (0,)), ((), ())),
            precision=HIGHEST, preferred_element_type=F32,
        )
        out_ref[:, c * BOXES : (c + 1) * BOXES] = direct + pushed


LIMIT = 48 * 1024 * 1024
VMEM = pl.BlockSpec(memory_space=pltpu.VMEM)


def shards(leaf_nodes, compress, expand, transfer, m2l_table):
    node_count = leaf_nodes.shape[0]
    grid_rows = lax.axis_size("horiz") // GRID_X
    parents = jnp.asarray(parent_selection())
    fine, coarse, halo = pl.pallas_call(
        functools.partial(charges_kernel, grid_rows),
        out_shape=[
            jax.ShapeDtypeStruct((BOXES, 256), F32),
            jax.ShapeDtypeStruct((COARSE_ROWS, 256), F32),
            jax.ShapeDtypeStruct((8, RIM_ROWS, 256), F32),
        ],
        in_specs=[VMEM] * 4,
        out_specs=[VMEM] * 3,
        scratch_shapes=[
            pltpu.VMEM((8, RIM_ROWS, 256), F32),
            pltpu.SemaphoreType.DMA((8,)),
            pltpu.SemaphoreType.DMA((8,)),
        ],
        compiler_params=pltpu.CompilerParams(
            collective_id=0, has_side_effects=True, vmem_limit_bytes=LIMIT
        ),
        name="charges",
    )(leaf_nodes.reshape(node_count, -1), compress, transfer, parents)
    high, low = pl.pallas_call(
        weights_kernel,
        out_shape=[jax.ShapeDtypeStruct((42, 192, 128), BF16)] * 2,
        in_specs=[VMEM] * 2,
        out_specs=[VMEM] * 2,
        scratch_shapes=[
            pltpu.VMEM((8 * 56, 1024), F32),
            pltpu.VMEM((56 * 32, 128), F32),
            pltpu.VMEM((56 * 32, 128), F32),
        ],
        compiler_params=pltpu.CompilerParams(vmem_limit_bytes=LIMIT),
        name="weights",
    )(m2l_table, jnp.asarray(table_selection()))
    result = pl.pallas_call(
        field_kernel,
        out_shape=jax.ShapeDtypeStruct((node_count, 8 * BOXES), F32),
        in_specs=[VMEM] * 8,
        out_specs=VMEM,
        scratch_shapes=[
            pltpu.VMEM((PX + 2, PY + 2, PZ + 16, 256), F32),
            pltpu.VMEM((PX // 2 + 2, PY // 2 + 2, COARSE_Z + 16, 256), F32),
            pltpu.VMEM((3, (PX + 2) * PY * PZ, 768), BF16),
            pltpu.VMEM((3, (PX + 2) * PY * PZ, 768), BF16),
            pltpu.VMEM((9, COARSE_ROWS, 768), BF16),
            pltpu.VMEM((9, COARSE_ROWS, 768), BF16),
            pltpu.VMEM((BOXES + COARSE_ROWS, 256), F32),
        ],
        compiler_params=pltpu.CompilerParams(vmem_limit_bytes=LIMIT),
        name="field",
    )(fine, coarse, halo, high, low, expand, transfer, parents)
    return result.reshape(node_count, 1, -1)


def solution(mesh):
    return jax.shard_map(
        shards,
        mesh=mesh,
        in_specs=(P("groups", "horiz", None), P(), P(), P(), P()),
        out_specs=P("groups", "horiz", None),
        check_vma=False,
    )
```

```python
import functools

import jax
import jax.numpy as jnp
import ml_dtypes
import numpy as np
from jax import lax
from jax.experimental import pallas as pl
from jax.experimental.pallas import tpu as pltpu
from jax.sharding import PartitionSpec as P

GRID_X = 8
PX = 4
PY = 4
PZ = 24
BOXES = PX * PY * PZ
COARSE_Z = 16
COARSE_ROWS = (PX // 2) * (PY // 2) * COARSE_Z
HIGHEST = lax.Precision.HIGHEST
BF16 = jnp.bfloat16
F32 = jnp.float32
DIRECTIONS = [(0, -1), (0, 1), (-1, 0), (1, 0), (-1, -1), (-1, 1), (1, -1), (1, 1)]
RIM_ROWS = PX * PZ + (PX // 2) * COARSE_Z
NT = (((1,), (1,)), ((), ()))


def table_selection():
    select = np.zeros((8 * 56, 316), np.float32)
    row = 0
    for dx in range(7):
        for dy in range(7):
            for dz in range(7):
                if max(abs(dx - 3), abs(dy - 3), abs(dz - 3)) >= 2:
                    select[dz * 56 + dx * 7 + dy, row] = 1.0
                    row += 1
    return select.astype(ml_dtypes.bfloat16)


def parent_selection():
    select = np.zeros((8 * COARSE_ROWS, BOXES), np.float32)
    for bx in range(PX):
        for by in range(PY):
            for bz in range(PZ):
                child = 4 * (bx % 2) + 2 * (by % 2) + bz % 2
                parent = ((bx // 2) * (PY // 2) + by // 2) * COARSE_Z + bz // 2
                select[child * COARSE_ROWS + parent, (bx * PY + by) * PZ + bz] = 1.0
    return select.astype(ml_dtypes.bfloat16)


def split(value):
    high = value.astype(BF16)
    return high, (value - high.astype(F32)).astype(BF16)


def select_dot(value, select, dims):
    high, low = split(value)
    return lax.dot_general(high, select, dims, preferred_element_type=F32) + lax.dot_general(
        low, select, dims, preferred_element_type=F32
    )


def build_weights(table_ref, select_ref, high_ref, low_ref, cube, lanes_a, lanes_b):
    table_high, table_low = split(table_ref[...])
    select = select_ref[...]
    cube[...] = jnp.dot(select, table_high, preferred_element_type=F32) + jnp.dot(
        select, table_low, preferred_element_type=F32
    )
    slot = lax.broadcasted_iota(jnp.int32, (56, 128), 1) // 32
    for half, out in enumerate((lanes_a, lanes_b)):
        for tile in range(8):
            parts = [
                cube[(4 * half + k) * 56 : (4 * half + k + 1) * 56, tile * 128 : (tile + 1) * 128]
                for k in range(4)
            ]
            for inner in range(4):
                merged = None
                for k in range(4):
                    by = (k - inner) % 4 * 32
                    moved = pltpu.roll(parts[k], by, 1) if by else parts[k]
                    merged = moved if merged is None else jnp.where(slot == k, moved, merged)
                out[pl.ds(tile * 4 + inner, 56, stride=32), :] = merged
    low_half = lax.broadcasted_iota(jnp.int32, (192, 128), 1) < 64
    lane = lax.broadcasted_iota(jnp.int32, (224, 128), 1)
    for dx in range(7):
        even0 = lanes_a[dx * 224 : (dx + 1) * 224, :]
        even1 = lanes_b[dx * 224 : (dx + 1) * 224, :]
        turned0 = pltpu.roll(even0, 96, 1)
        turned1 = pltpu.roll(even1, 96, 1)
        odd0 = jnp.where(lane < 96, turned0, turned1)
        odd1 = turned1
        for w, (source, straight) in enumerate(
            ((even0, True), (odd0, True), (even0, False), (odd0, False), (even1, True), (odd1, True))
        ):
            other = pltpu.roll(source, 64, 1)
            first, second = (source, other) if straight else (other, source)
            high, low = split(jnp.where(low_half, first[:192], second[32:]))
            high_ref[w * 7 + dx] = high
            low_ref[w * 7 + dx] = low


def charges_kernel(
    grid_rows, leaf_hbm, compress_hbm, transfer_hbm, parents_hbm, table_hbm, spread_hbm,
    fine_ref, coarse_ref, halo_ref, high_ref, low_ref,
    leaf_ref, compress_ref, transfer_ref, parents_ref, table_ref, spread_ref,
    cube, lanes_a, lanes_b, rim, load_sem, send_sem, recv_sem,
):
    loads = [
        pltpu.make_async_copy(source, target, load_sem.at[number])
        for number, (source, target) in enumerate(
            (
                (compress_hbm, compress_ref),
                (transfer_hbm, transfer_ref),
                (leaf_hbm.at[:, 0, :], leaf_ref),
                (parents_hbm, parents_ref),
                (table_hbm, table_ref),
                (spread_hbm, spread_ref),
            )
        )
    ]
    for load in loads:
        load.start()
    here = lax.axis_index("horiz")
    tile_x = here // grid_rows
    tile_y = here % grid_rows

    def present(dx, dy):
        x, y = tile_x + dx, tile_y + dy
        return (x >= 0) & (x < GRID_X) & (y >= 0) & (y < grid_rows)

    barrier = pltpu.get_barrier_semaphore()
    for dx, dy in DIRECTIONS:
        @pl.when(present(dx, dy))
        def _(dx=dx, dy=dy):
            pl.semaphore_signal(
                barrier, inc=1, device_id={"horiz": here + dx * grid_rows + dy},
                device_id_type=pl.DeviceIdType.MESH,
            )

    loads[0].wait()
    loads[1].wait()
    compress = compress_ref[...]
    both = jnp.dot(compress, transfer_ref[...], precision=HIGHEST, preferred_element_type=F32)
    loads[2].wait()
    fine, coarse = [], None
    for child in range(8):
        high, low = split(leaf_ref[:, child * BOXES : (child + 1) * BOXES])
        onto = jnp.concatenate([compress, both[:, child * 64 : (child + 1) * 64]], axis=0)
        onto_high, onto_low = split(onto)
        charged = jnp.dot(
            jnp.concatenate([onto_high, onto_low, onto_high], axis=1),
            jnp.concatenate([high, high, low], axis=0),
            preferred_element_type=F32,
        )
        fine.append(charged[:32])
        coarse = charged[32:] if coarse is None else coarse + charged[32:]
    fine_ref[...] = jnp.concatenate(fine, axis=0).T
    loads[3].wait()
    grouped = select_dot(coarse, parents_ref[...], NT)
    coarse_ref[...] = jnp.concatenate(
        [grouped[:, c * COARSE_ROWS : (c + 1) * COARSE_ROWS] for c in range(8)], axis=0
    ).T

    def pick(step, extent):
        return range(extent) if step == 0 else ([extent - 1] if step > 0 else [0])

    lengths = []
    for number, (dx, dy) in enumerate(DIRECTIONS):
        at = 0
        for x in pick(dx, PX):
            for y in pick(dy, PY):
                start = (x * PY + y) * PZ
                rim[number, at : at + PZ, :] = fine_ref[start : start + PZ, :]
                at += PZ
        for x in pick(dx, PX // 2):
            for y in pick(dy, PY // 2):
                start = (x * (PY // 2) + y) * COARSE_Z
                rim[number, at : at + COARSE_Z, :] = coarse_ref[start : start + COARSE_Z, :]
                at += COARSE_Z
        lengths.append(at)

    peers = sum(jnp.where(present(dx, dy), 1, 0) for dx, dy in DIRECTIONS)
    pl.semaphore_wait(barrier, peers)

    def copy_of(number):
        dx, dy = DIRECTIONS[number]
        return pltpu.make_async_remote_copy(
            src_ref=rim.at[number, pl.ds(0, lengths[number])],
            dst_ref=halo_ref.at[number, pl.ds(0, lengths[number])],
            send_sem=send_sem.at[number],
            recv_sem=recv_sem.at[number],
            device_id={"horiz": here + dx * grid_rows + dy},
            device_id_type=pl.DeviceIdType.MESH,
        )

    for number, (dx, dy) in enumerate(DIRECTIONS):
        @pl.when(present(dx, dy))
        def _(number=number):
            copy_of(number).start()

    for number, (dx, dy) in enumerate(DIRECTIONS):
        @pl.when(jnp.logical_not(present(-dx, -dy)))
        def _(number=number):
            halo_ref[number] = jnp.zeros(halo_ref.shape[1:], F32)

    loads[4].wait()
    loads[5].wait()
    build_weights(table_ref, spread_ref, high_ref, low_ref, cube, lanes_a, lanes_b)

    for number, (dx, dy) in enumerate(DIRECTIONS):
        @pl.when(present(dx, dy))
        def _(number=number):
            copy_of(number).wait_send()

        @pl.when(present(-dx, -dy))
        def _(number=number):
            copy_of(number).wait_recv()


def field_kernel(
    fine_ref, coarse_ref, halo_ref, high_ref, low_ref, expand_hbm, transfer_hbm, parents_hbm, out_hbm,
    wide, wide_coarse, wins_high, wins_low, cwins_high, cwins_low, total,
    expand_ref, transfer_ref, parents_ref, out_ref, load_sem, store_sem,
):
    loads = [
        pltpu.make_async_copy(source, target, load_sem.at[number])
        for number, (source, target) in enumerate(
            (
                (expand_hbm, expand_ref),
                (transfer_hbm, transfer_ref),
                (parents_hbm, parents_ref),
            )
        )
    ]
    for load in loads:
        load.start()
    zero_rows = jnp.zeros((8, 256), F32)

    def place(x, y, rows):
        wide[x, y, 0:8, :] = zero_rows
        wide[x, y, 8 : 8 + PZ, :] = rows
        wide[x, y, 8 + PZ : 16 + PZ, :] = zero_rows

    def place_coarse(x, y, rows):
        wide_coarse[x, y, 0:8, :] = zero_rows
        wide_coarse[x, y, 8 : 8 + COARSE_Z, :] = rows
        wide_coarse[x, y, 8 + COARSE_Z : 16 + COARSE_Z, :] = zero_rows

    for x in range(PX):
        for y in range(PY):
            start = (x * PY + y) * PZ
            place(x + 1, y + 1, fine_ref[start : start + PZ, :])
    for x in range(PX // 2):
        for y in range(PY // 2):
            start = (x * (PY // 2) + y) * COARSE_Z
            place_coarse(x + 1, y + 1, coarse_ref[start : start + COARSE_Z, :])

    def rim_places(step, extent):
        return range(1, extent + 1) if step == 0 else ([0] if step > 0 else [extent + 1])

    for number, (dx, dy) in enumerate(DIRECTIONS):
        at = 0
        for x in rim_places(dx, PX):
            for y in rim_places(dy, PY):
                place(x, y, halo_ref[number, at : at + PZ, :])
                at += PZ
        for x in rim_places(dx, PX // 2):
            for y in rim_places(dy, PY // 2):
                place_coarse(x, y, halo_ref[number, at : at + COARSE_Z, :])
                at += COARSE_Z

    span = PY * PZ
    for sy in range(3):
        for sz in range(3):
            for x in range(PX + 2):
                rows = jnp.concatenate(
                    [wide[x, sy + y, 7 + sz : 7 + sz + PZ, :] for y in range(PY)], axis=0
                )
                high, low = split(rows)
                wins_high[sy, x * span : (x + 1) * span, sz * 256 : (sz + 1) * 256] = high
                wins_low[sy, x * span : (x + 1) * span, sz * 256 : (sz + 1) * 256] = low
            for sx in range(3):
                rows = jnp.concatenate(
                    [
                        wide_coarse[sx + x, sy + y, 7 + sz : 7 + sz + COARSE_Z, :]
                        for x in range(PX // 2)
                        for y in range(PY // 2)
                    ],
                    axis=0,
                )
                high, low = split(rows)
                cwins_high[sx * 3 + sy, :, sz * 256 : (sz + 1) * 256] = high
                cwins_low[sx * 3 + sy, :, sz * 256 : (sz + 1) * 256] = low

    total[...] = jnp.zeros_like(total)

    def weight(ref, sx, sy, sz):
        rows = []
        for target in range(8):
            tx, ty, tz = target >> 2, target >> 1 & 1, target & 1
            at_y = pl.multiple_of((2 * sy + 1 - ty) * 32, 32)
            first = (2 * sz + 1 - tz) * 7 + 2 * sx + 1 - tx
            rows.append(
                jnp.concatenate(
                    [ref[first, pl.ds(at_y, 32), :], ref[first + 1, pl.ds(at_y, 32), :]], axis=1
                )
            )
        return jnp.concatenate(rows, axis=0)

    def step(at, carry):
        sx, sy = at // 3, at % 3
        rows = pl.ds(pl.multiple_of(sx * span, 32), PX * span)
        high = jnp.concatenate([wins_high[sy, rows, :], cwins_high[at]], axis=0)
        low = jnp.concatenate([wins_low[sy, rows, :], cwins_low[at]], axis=0)
        by_high = jnp.concatenate([weight(high_ref, sx, sy, sz) for sz in range(3)], axis=1)
        by_low = jnp.concatenate([weight(low_ref, sx, sy, sz) for sz in range(3)], axis=1)
        total[...] += lax.dot_general(
            jnp.concatenate([high, low, high], axis=1),
            jnp.concatenate([by_high, by_high, by_low], axis=1),
            NT,
            preferred_element_type=F32,
        )
        return carry

    lax.fori_loop(0, 9, step, 0)

    for load in loads:
        load.wait()
    expand = expand_ref[...].T
    pushes = lax.dot_general(
        transfer_ref[...], expand, (((0,), (0,)), ((), ())), precision=HIGHEST,
        preferred_element_type=F32,
    )
    expand_high, expand_low = split(jnp.concatenate([expand] * 8, axis=1))
    push_high, push_low = split(pushes)
    child_of = lax.broadcasted_iota(jnp.int32, (64, 256), 1) // 32
    nothing = jnp.zeros((64, 256), BF16)
    spread_high = jnp.concatenate([jnp.where(child_of == c, expand_high, nothing) for c in range(8)])
    spread_low = jnp.concatenate([jnp.where(child_of == c, expand_low, nothing) for c in range(8)])

    across = (0.5 * total[BOXES:, :]).T
    across = jnp.concatenate([across[c * 32 : (c + 1) * 32] for c in range(8)], axis=1)
    coarse_field = select_dot(across, parents_ref[...], (((1,), (0,)), ((), ())))
    coarse_high, coarse_low = split(coarse_field)
    field_high, field_low = split(total[:BOXES, :])
    local = lax.dot_general(
        jnp.concatenate([spread_high, spread_low, spread_high], axis=1),
        jnp.concatenate([field_high, field_high, field_low], axis=1),
        NT,
        preferred_element_type=F32,
    ) + jnp.dot(
        jnp.concatenate([push_high, push_low, push_high], axis=1),
        jnp.concatenate([coarse_high, coarse_high, coarse_low], axis=0),
        preferred_element_type=F32,
    )
    stores = []
    for c in range(8):
        out_ref[:, c * BOXES : (c + 1) * BOXES] = local[c * 64 : (c + 1) * 64]
        stores.append(
            pltpu.make_async_copy(
                out_ref.at[:, pl.ds(c * BOXES, BOXES)],
                out_hbm.at[:, 0, pl.ds(c * BOXES, BOXES)],
                store_sem.at[c],
            )
        )
        stores[c].start()
    for store in stores:
        store.wait()


LIMIT = 24 * 1024 * 1024
VMEM = pl.BlockSpec(memory_space=pltpu.VMEM)
HBM = pl.BlockSpec(memory_space=pltpu.HBM)


def shards(leaf_nodes, compress, expand, transfer, m2l_table):
    node_count = leaf_nodes.shape[0]
    grid_rows = lax.axis_size("horiz") // GRID_X
    parents = jnp.asarray(parent_selection())
    spread = jnp.asarray(table_selection())
    fine, coarse, halo, high, low = pl.pallas_call(
        functools.partial(charges_kernel, grid_rows),
        out_shape=[
            jax.ShapeDtypeStruct((BOXES, 256), F32),
            jax.ShapeDtypeStruct((COARSE_ROWS, 256), F32),
            jax.ShapeDtypeStruct((8, RIM_ROWS, 256), F32),
            jax.ShapeDtypeStruct((42, 192, 128), BF16),
            jax.ShapeDtypeStruct((42, 192, 128), BF16),
        ],
        in_specs=[HBM] * 6,
        out_specs=[VMEM] * 5,
        scratch_shapes=[
            pltpu.VMEM((node_count, 8 * BOXES), F32),
            pltpu.VMEM(compress.shape, F32),
            pltpu.VMEM(transfer.shape, F32),
            pltpu.VMEM(parents.shape, BF16),
            pltpu.VMEM(m2l_table.shape, F32),
            pltpu.VMEM(spread.shape, BF16),
            pltpu.VMEM((8 * 56, 1024), F32),
            pltpu.VMEM((56 * 32, 128), F32),
            pltpu.VMEM((56 * 32, 128), F32),
            pltpu.VMEM((8, RIM_ROWS, 256), F32),
            pltpu.SemaphoreType.DMA((6,)),
            pltpu.SemaphoreType.DMA((8,)),
            pltpu.SemaphoreType.DMA((8,)),
        ],
        compiler_params=pltpu.CompilerParams(
            collective_id=0, has_side_effects=True, vmem_limit_bytes=LIMIT
        ),
        name="charges",
    )(leaf_nodes, compress, transfer, parents, m2l_table, spread)
    return pl.pallas_call(
        field_kernel,
        out_shape=jax.ShapeDtypeStruct(leaf_nodes.shape, F32),
        in_specs=[VMEM] * 5 + [HBM] * 3,
        out_specs=HBM,
        scratch_shapes=[
            pltpu.VMEM((PX + 2, PY + 2, PZ + 16, 256), F32),
            pltpu.VMEM((PX // 2 + 2, PY // 2 + 2, COARSE_Z + 16, 256), F32),
            pltpu.VMEM((3, (PX + 2) * PY * PZ, 768), BF16),
            pltpu.VMEM((3, (PX + 2) * PY * PZ, 768), BF16),
            pltpu.VMEM((9, COARSE_ROWS, 768), BF16),
            pltpu.VMEM((9, COARSE_ROWS, 768), BF16),
            pltpu.VMEM((BOXES + COARSE_ROWS, 256), F32),
            pltpu.VMEM(expand.shape[::-1], F32),
            pltpu.VMEM(transfer.shape, F32),
            pltpu.VMEM(parents.shape, BF16),
            pltpu.VMEM((node_count, 8 * BOXES), F32),
            pltpu.SemaphoreType.DMA((3,)),
            pltpu.SemaphoreType.DMA((8,)),
        ],
        compiler_params=pltpu.CompilerParams(vmem_limit_bytes=LIMIT),
        name="field",
    )(fine, coarse, halo, high, low, expand.T, transfer, parents)


def solution(mesh):
    return jax.shard_map(
        shards,
        mesh=mesh,
        in_specs=(P("groups", "horiz", None), P(), P(), P(), P()),
        out_specs=P("groups", "horiz", None),
        check_vma=False,
    )
```

```python
import functools

import jax
import jax.numpy as jnp
import ml_dtypes
import numpy as np
from jax import lax
from jax.experimental import pallas as pl
from jax.experimental.pallas import tpu as pltpu
from jax.sharding import PartitionSpec as P

GRID_X = 8
PX = 4
PY = 4
PZ = 24
BOXES = PX * PY * PZ
COARSE_Z = 16
COARSE_ROWS = (PX // 2) * (PY // 2) * COARSE_Z
HIGHEST = lax.Precision.HIGHEST
BF16 = jnp.bfloat16
F32 = jnp.float32
DIRECTIONS = [(0, -1), (0, 1), (-1, 0), (1, 0), (-1, -1), (-1, 1), (1, -1), (1, 1)]
RIM_ROWS = PX * PZ + (PX // 2) * COARSE_Z
NT = (((1,), (1,)), ((), ()))


def table_selection():
    select = np.zeros((8 * 56, 316), np.float32)
    row = 0
    for dx in range(7):
        for dy in range(7):
            for dz in range(7):
                if max(abs(dx - 3), abs(dy - 3), abs(dz - 3)) >= 2:
                    select[dz * 56 + dx * 7 + dy, row] = 1.0
                    row += 1
    return select.astype(ml_dtypes.bfloat16)


def parent_selection():
    select = np.zeros((8 * COARSE_ROWS, BOXES), np.float32)
    for bx in range(PX):
        for by in range(PY):
            for bz in range(PZ):
                child = 4 * (bx % 2) + 2 * (by % 2) + bz % 2
                parent = ((bx // 2) * (PY // 2) + by // 2) * COARSE_Z + bz // 2
                select[child * COARSE_ROWS + parent, (bx * PY + by) * PZ + bz] = 1.0
    return select.astype(ml_dtypes.bfloat16)


def split(value):
    high = value.astype(BF16)
    return high, (value - high.astype(F32)).astype(BF16)


def select_dot(value, select, dims):
    high, low = split(value)
    return lax.dot_general(high, select, dims, preferred_element_type=F32) + lax.dot_general(
        low, select, dims, preferred_element_type=F32
    )


def build_weights(table_ref, select_ref, high_ref, low_ref, cube, lanes_a, lanes_b):
    table_high, table_low = split(table_ref[...])
    select = select_ref[...]
    cube[...] = jnp.dot(select, table_high, preferred_element_type=F32) + jnp.dot(
        select, table_low, preferred_element_type=F32
    )
    slot = lax.broadcasted_iota(jnp.int32, (56, 128), 1) // 32
    for half, out in enumerate((lanes_a, lanes_b)):
        for tile in range(8):
            parts = [
                cube[(4 * half + k) * 56 : (4 * half + k + 1) * 56, tile * 128 : (tile + 1) * 128]
                for k in range(4)
            ]
            for inner in range(4):
                merged = None
                for k in range(4):
                    by = (k - inner) % 4 * 32
                    moved = pltpu.roll(parts[k], by, 1) if by else parts[k]
                    merged = moved if merged is None else jnp.where(slot == k, moved, merged)
                out[pl.ds(tile * 4 + inner, 56, stride=32), :] = merged
    low_half = lax.broadcasted_iota(jnp.int32, (192, 128), 1) < 64
    lane = lax.broadcasted_iota(jnp.int32, (224, 128), 1)
    for dx in range(7):
        even0 = lanes_a[dx * 224 : (dx + 1) * 224, :]
        even1 = lanes_b[dx * 224 : (dx + 1) * 224, :]
        turned0 = pltpu.roll(even0, 96, 1)
        turned1 = pltpu.roll(even1, 96, 1)
        odd0 = jnp.where(lane < 96, turned0, turned1)
        odd1 = turned1
        for w, (source, straight) in enumerate(
            ((even0, True), (odd0, True), (even0, False), (odd0, False), (even1, True), (odd1, True))
        ):
            other = pltpu.roll(source, 64, 1)
            first, second = (source, other) if straight else (other, source)
            high, low = split(jnp.where(low_half, first[:192], second[32:]))
            high_ref[w * 7 + dx] = high
            low_ref[w * 7 + dx] = low


def far_kernel(
    grid_rows, leaf_hbm, compress_hbm, transfer_hbm, parents_hbm, table_hbm, spread_hbm,
    expand_hbm, out_hbm, fine_ref, coarse_ref, halo_ref, high_ref, low_ref,
    leaf_ref, compress_ref, transfer_ref, parents_ref, table_ref, spread_ref,
    cube, lanes_a, lanes_b, rim, load_sem, send_sem, recv_sem,
    wide, wide_coarse, wins_high, wins_low, cwins_high, cwins_low, total,
    expand_ref, out_ref, store_sem,
):
    loads = [
        pltpu.make_async_copy(source, target, load_sem.at[number])
        for number, (source, target) in enumerate(
            (
                (compress_hbm, compress_ref),
                (transfer_hbm, transfer_ref),
                (leaf_hbm.at[:, 0, :], leaf_ref),
                (parents_hbm, parents_ref),
                (table_hbm, table_ref),
                (spread_hbm, spread_ref),
                (expand_hbm, expand_ref),
            )
        )
    ]
    for load in loads:
        load.start()
    here = lax.axis_index("horiz")
    tile_x = here // grid_rows
    tile_y = here % grid_rows

    def present(dx, dy):
        x, y = tile_x + dx, tile_y + dy
        return (x >= 0) & (x < GRID_X) & (y >= 0) & (y < grid_rows)

    barrier = pltpu.get_barrier_semaphore()
    for dx, dy in DIRECTIONS:
        @pl.when(present(dx, dy))
        def _(dx=dx, dy=dy):
            pl.semaphore_signal(
                barrier, inc=1, device_id={"horiz": here + dx * grid_rows + dy},
                device_id_type=pl.DeviceIdType.MESH,
            )

    loads[0].wait()
    loads[1].wait()
    compress = compress_ref[...]
    both = jnp.dot(compress, transfer_ref[...], precision=HIGHEST, preferred_element_type=F32)
    loads[2].wait()
    fine, coarse = [], None
    for child in range(8):
        high, low = split(leaf_ref[:, child * BOXES : (child + 1) * BOXES])
        onto = jnp.concatenate([compress, both[:, child * 64 : (child + 1) * 64]], axis=0)
        onto_high, onto_low = split(onto)
        charged = jnp.dot(
            jnp.concatenate([onto_high, onto_low, onto_high], axis=1),
            jnp.concatenate([high, high, low], axis=0),
            preferred_element_type=F32,
        )
        fine.append(charged[:32])
        coarse = charged[32:] if coarse is None else coarse + charged[32:]
    fine_ref[...] = jnp.concatenate(fine, axis=0).T
    loads[3].wait()
    grouped = select_dot(coarse, parents_ref[...], NT)
    coarse_ref[...] = jnp.concatenate(
        [grouped[:, c * COARSE_ROWS : (c + 1) * COARSE_ROWS] for c in range(8)], axis=0
    ).T

    def pick(step, extent):
        return range(extent) if step == 0 else ([extent - 1] if step > 0 else [0])

    lengths = []
    for number, (dx, dy) in enumerate(DIRECTIONS):
        at = 0
        for x in pick(dx, PX):
            for y in pick(dy, PY):
                start = (x * PY + y) * PZ
                rim[number, at : at + PZ, :] = fine_ref[start : start + PZ, :]
                at += PZ
        for x in pick(dx, PX // 2):
            for y in pick(dy, PY // 2):
                start = (x * (PY // 2) + y) * COARSE_Z
                rim[number, at : at + COARSE_Z, :] = coarse_ref[start : start + COARSE_Z, :]
                at += COARSE_Z
        lengths.append(at)

    peers = sum(jnp.where(present(dx, dy), 1, 0) for dx, dy in DIRECTIONS)
    pl.semaphore_wait(barrier, peers)

    def copy_of(number):
        dx, dy = DIRECTIONS[number]
        return pltpu.make_async_remote_copy(
            src_ref=rim.at[number, pl.ds(0, lengths[number])],
            dst_ref=halo_ref.at[number, pl.ds(0, lengths[number])],
            send_sem=send_sem.at[number],
            recv_sem=recv_sem.at[number],
            device_id={"horiz": here + dx * grid_rows + dy},
            device_id_type=pl.DeviceIdType.MESH,
        )

    for number, (dx, dy) in enumerate(DIRECTIONS):
        @pl.when(present(dx, dy))
        def _(number=number):
            copy_of(number).start()

    for number, (dx, dy) in enumerate(DIRECTIONS):
        @pl.when(jnp.logical_not(present(-dx, -dy)))
        def _(number=number):
            halo_ref[number] = jnp.zeros(halo_ref.shape[1:], F32)

    loads[4].wait()
    loads[5].wait()
    build_weights(table_ref, spread_ref, high_ref, low_ref, cube, lanes_a, lanes_b)

    zero_rows = jnp.zeros((8, 256), F32)

    def place(x, y, rows):
        wide[x, y, 0:8, :] = zero_rows
        wide[x, y, 8 : 8 + PZ, :] = rows
        wide[x, y, 8 + PZ : 16 + PZ, :] = zero_rows

    def place_coarse(x, y, rows):
        wide_coarse[x, y, 0:8, :] = zero_rows
        wide_coarse[x, y, 8 : 8 + COARSE_Z, :] = rows
        wide_coarse[x, y, 8 + COARSE_Z : 16 + COARSE_Z, :] = zero_rows

    for x in range(PX):
        for y in range(PY):
            start = (x * PY + y) * PZ
            place(x + 1, y + 1, fine_ref[start : start + PZ, :])
    for x in range(PX // 2):
        for y in range(PY // 2):
            start = (x * (PY // 2) + y) * COARSE_Z
            place_coarse(x + 1, y + 1, coarse_ref[start : start + COARSE_Z, :])

    for number, (dx, dy) in enumerate(DIRECTIONS):
        @pl.when(present(dx, dy))
        def _(number=number):
            copy_of(number).wait_send()

        @pl.when(present(-dx, -dy))
        def _(number=number):
            copy_of(number).wait_recv()

    def rim_places(step, extent):
        return range(1, extent + 1) if step == 0 else ([0] if step > 0 else [extent + 1])

    for number, (dx, dy) in enumerate(DIRECTIONS):
        at = 0
        for x in rim_places(dx, PX):
            for y in rim_places(dy, PY):
                place(x, y, halo_ref[number, at : at + PZ, :])
                at += PZ
        for x in rim_places(dx, PX // 2):
            for y in rim_places(dy, PY // 2):
                place_coarse(x, y, halo_ref[number, at : at + COARSE_Z, :])
                at += COARSE_Z

    span = PY * PZ
    for sy in range(3):
        for sz in range(3):
            for x in range(PX + 2):
                rows = jnp.concatenate(
                    [wide[x, sy + y, 7 + sz : 7 + sz + PZ, :] for y in range(PY)], axis=0
                )
                high, low = split(rows)
                wins_high[sy, x * span : (x + 1) * span, sz * 256 : (sz + 1) * 256] = high
                wins_low[sy, x * span : (x + 1) * span, sz * 256 : (sz + 1) * 256] = low
            for sx in range(3):
                rows = jnp.concatenate(
                    [
                        wide_coarse[sx + x, sy + y, 7 + sz : 7 + sz + COARSE_Z, :]
                        for x in range(PX // 2)
                        for y in range(PY // 2)
                    ],
                    axis=0,
                )
                high, low = split(rows)
                cwins_high[sx * 3 + sy, :, sz * 256 : (sz + 1) * 256] = high
                cwins_low[sx * 3 + sy, :, sz * 256 : (sz + 1) * 256] = low

    total[...] = jnp.zeros_like(total)

    def weight(ref, sx, sy, sz):
        rows = []
        for target in range(8):
            tx, ty, tz = target >> 2, target >> 1 & 1, target & 1
            at_y = pl.multiple_of((2 * sy + 1 - ty) * 32, 32)
            first = (2 * sz + 1 - tz) * 7 + 2 * sx + 1 - tx
            rows.append(
                jnp.concatenate(
                    [ref[first, pl.ds(at_y, 32), :], ref[first + 1, pl.ds(at_y, 32), :]], axis=1
                )
            )
        return jnp.concatenate(rows, axis=0)

    def step(at, carry):
        sx, sy = at // 3, at % 3
        rows = pl.ds(pl.multiple_of(sx * span, 32), PX * span)
        high = jnp.concatenate([wins_high[sy, rows, :], cwins_high[at]], axis=0)
        low = jnp.concatenate([wins_low[sy, rows, :], cwins_low[at]], axis=0)
        by_high = jnp.concatenate([weight(high_ref, sx, sy, sz) for sz in range(3)], axis=1)
        by_low = jnp.concatenate([weight(low_ref, sx, sy, sz) for sz in range(3)], axis=1)
        total[...] += lax.dot_general(
            jnp.concatenate([high, low, high], axis=1),
            jnp.concatenate([by_high, by_high, by_low], axis=1),
            NT,
            preferred_element_type=F32,
        )
        return carry

    lax.fori_loop(0, 9, step, 0)

    loads[6].wait()
    expand = expand_ref[...].T
    pushes = lax.dot_general(
        transfer_ref[...], expand, (((0,), (0,)), ((), ())), precision=HIGHEST,
        preferred_element_type=F32,
    )
    expand_high, expand_low = split(jnp.concatenate([expand] * 8, axis=1))
    push_high, push_low = split(pushes)
    child_of = lax.broadcasted_iota(jnp.int32, (64, 256), 1) // 32
    nothing = jnp.zeros((64, 256), BF16)
    spread_high = jnp.concatenate([jnp.where(child_of == c, expand_high, nothing) for c in range(8)])
    spread_low = jnp.concatenate([jnp.where(child_of == c, expand_low, nothing) for c in range(8)])

    across = (0.5 * total[BOXES:, :]).T
    across = jnp.concatenate([across[c * 32 : (c + 1) * 32] for c in range(8)], axis=1)
    coarse_field = select_dot(across, parents_ref[...], (((1,), (0,)), ((), ())))
    coarse_high, coarse_low = split(coarse_field)
    field_high, field_low = split(total[:BOXES, :])
    local = lax.dot_general(
        jnp.concatenate([spread_high, spread_low, spread_high], axis=1),
        jnp.concatenate([field_high, field_high, field_low], axis=1),
        NT,
        preferred_element_type=F32,
    ) + jnp.dot(
        jnp.concatenate([push_high, push_low, push_high], axis=1),
        jnp.concatenate([coarse_high, coarse_high, coarse_low], axis=0),
        preferred_element_type=F32,
    )
    stores = []
    for c in range(8):
        out_ref[:, c * BOXES : (c + 1) * BOXES] = local[c * 64 : (c + 1) * 64]
        stores.append(
            pltpu.make_async_copy(
                out_ref.at[:, pl.ds(c * BOXES, BOXES)],
                out_hbm.at[:, 0, pl.ds(c * BOXES, BOXES)],
                store_sem.at[c],
            )
        )
        stores[c].start()
    for store in stores:
        store.wait()


LIMIT = 58 * 1024 * 1024
HBM = pl.BlockSpec(memory_space=pltpu.HBM)


def shards(leaf_nodes, compress, expand, transfer, m2l_table):
    node_count = leaf_nodes.shape[0]
    grid_rows = lax.axis_size("horiz") // GRID_X
    parents = jnp.asarray(parent_selection())
    spread = jnp.asarray(table_selection())
    return pl.pallas_call(
        functools.partial(far_kernel, grid_rows),
        out_shape=jax.ShapeDtypeStruct(leaf_nodes.shape, F32),
        in_specs=[HBM] * 7,
        out_specs=HBM,
        scratch_shapes=[
            pltpu.VMEM((BOXES, 256), F32),
            pltpu.VMEM((COARSE_ROWS, 256), F32),
            pltpu.VMEM((8, RIM_ROWS, 256), F32),
            pltpu.VMEM((42, 192, 128), BF16),
            pltpu.VMEM((42, 192, 128), BF16),
            pltpu.VMEM((node_count, 8 * BOXES), F32),
            pltpu.VMEM(compress.shape, F32),
            pltpu.VMEM(transfer.shape, F32),
            pltpu.VMEM(parents.shape, BF16),
            pltpu.VMEM(m2l_table.shape, F32),
            pltpu.VMEM(spread.shape, BF16),
            pltpu.VMEM((8 * 56, 1024), F32),
            pltpu.VMEM((56 * 32, 128), F32),
            pltpu.VMEM((56 * 32, 128), F32),
            pltpu.VMEM((8, RIM_ROWS, 256), F32),
            pltpu.SemaphoreType.DMA((7,)),
            pltpu.SemaphoreType.DMA((8,)),
            pltpu.SemaphoreType.DMA((8,)),
            pltpu.VMEM((PX + 2, PY + 2, PZ + 16, 256), F32),
            pltpu.VMEM((PX // 2 + 2, PY // 2 + 2, COARSE_Z + 16, 256), F32),
            pltpu.VMEM((3, (PX + 2) * PY * PZ, 768), BF16),
            pltpu.VMEM((3, (PX + 2) * PY * PZ, 768), BF16),
            pltpu.VMEM((9, COARSE_ROWS, 768), BF16),
            pltpu.VMEM((9, COARSE_ROWS, 768), BF16),
            pltpu.VMEM((BOXES + COARSE_ROWS, 256), F32),
            pltpu.VMEM(expand.shape[::-1], F32),
            pltpu.VMEM((node_count, 8 * BOXES), F32),
            pltpu.SemaphoreType.DMA((8,)),
        ],
        compiler_params=pltpu.CompilerParams(
            collective_id=0, has_side_effects=True, vmem_limit_bytes=LIMIT
        ),
        name="far",
    )(leaf_nodes, compress, transfer, parents, m2l_table, spread, expand.T)


def solution(mesh):
    return jax.shard_map(
        shards,
        mesh=mesh,
        in_specs=(P("groups", "horiz", None), P(), P(), P(), P()),
        out_specs=P("groups", "horiz", None),
        check_vma=False,
    )
```

```python
import functools

import jax
import jax.numpy as jnp
import ml_dtypes
import numpy as np
from jax import lax
from jax.experimental import pallas as pl
from jax.experimental.pallas import tpu as pltpu
from jax.sharding import PartitionSpec as P

GRID_X = 8
PX = 4
PY = 4
PZ = 24
BOXES = PX * PY * PZ
COARSE_Z = 16
COARSE_ROWS = (PX // 2) * (PY // 2) * COARSE_Z
HIGHEST = lax.Precision.HIGHEST
BF16 = jnp.bfloat16
F32 = jnp.float32
DIRECTIONS = [(0, -1), (0, 1), (-1, 0), (1, 0), (-1, -1), (-1, 1), (1, -1), (1, 1)]
RIM_ROWS = PX * PZ + (PX // 2) * COARSE_Z
NT = (((1,), (1,)), ((), ()))


def table_selection():
    select = np.zeros((8 * 56, 316), np.float32)
    row = 0
    for dx in range(7):
        for dy in range(7):
            for dz in range(7):
                if max(abs(dx - 3), abs(dy - 3), abs(dz - 3)) >= 2:
                    select[dz * 56 + dx * 7 + dy, row] = 1.0
                    row += 1
    return select.astype(ml_dtypes.bfloat16)


def parent_selection():
    select = np.zeros((8 * COARSE_ROWS, BOXES), np.float32)
    for bx in range(PX):
        for by in range(PY):
            for bz in range(PZ):
                child = 4 * (bx % 2) + 2 * (by % 2) + bz % 2
                parent = ((bx // 2) * (PY // 2) + by // 2) * COARSE_Z + bz // 2
                select[child * COARSE_ROWS + parent, (bx * PY + by) * PZ + bz] = 1.0
    return select.astype(ml_dtypes.bfloat16)


def split(value):
    high = value.astype(BF16)
    return high, (value - high.astype(F32)).astype(BF16)


def select_dot(value, select, dims):
    high, low = split(value)
    return lax.dot_general(high, select, dims, preferred_element_type=F32) + lax.dot_general(
        low, select, dims, preferred_element_type=F32
    )


def build_weights(table_ref, select_ref, high_ref, low_ref, cube, lanes_a, lanes_b):
    table_high, table_low = split(table_ref[...])
    select = select_ref[...]
    cube[...] = jnp.dot(select, table_high, preferred_element_type=F32) + jnp.dot(
        select, table_low, preferred_element_type=F32
    )
    slot = lax.broadcasted_iota(jnp.int32, (56, 128), 1) // 32
    for half, out in enumerate((lanes_a, lanes_b)):
        for tile in range(8):
            parts = [
                cube[(4 * half + k) * 56 : (4 * half + k + 1) * 56, tile * 128 : (tile + 1) * 128]
                for k in range(4)
            ]
            for inner in range(4):
                merged = None
                for k in range(4):
                    by = (k - inner) % 4 * 32
                    moved = pltpu.roll(parts[k], by, 1) if by else parts[k]
                    merged = moved if merged is None else jnp.where(slot == k, moved, merged)
                out[pl.ds(tile * 4 + inner, 56, stride=32), :] = merged
    low_half = lax.broadcasted_iota(jnp.int32, (192, 128), 1) < 64
    lane = lax.broadcasted_iota(jnp.int32, (224, 128), 1)
    for dx in range(7):
        even0 = lanes_a[dx * 224 : (dx + 1) * 224, :]
        even1 = lanes_b[dx * 224 : (dx + 1) * 224, :]
        turned0 = pltpu.roll(even0, 96, 1)
        turned1 = pltpu.roll(even1, 96, 1)
        odd0 = jnp.where(lane < 96, turned0, turned1)
        odd1 = turned1
        for w, (source, straight) in enumerate(
            ((even0, True), (odd0, True), (even0, False), (odd0, False), (even1, True), (odd1, True))
        ):
            other = pltpu.roll(source, 64, 1)
            first, second = (source, other) if straight else (other, source)
            high, low = split(jnp.where(low_half, first[:192], second[32:]))
            high_ref[w * 7 + dx] = high
            low_ref[w * 7 + dx] = low


def far_kernel(
    grid_rows, leaf_hbm, compress_hbm, transfer_hbm, parents_hbm, table_hbm, spread_hbm,
    expand_hbm, out_hbm, fine_ref, coarse_ref, halo_ref, high_ref, low_ref,
    leaf_ref, compress_ref, transfer_ref, parents_ref, table_ref, spread_ref,
    cube, lanes_a, lanes_b, rim, load_sem, send_sem, recv_sem,
    wide, wide_coarse, wins_high, wins_low, total,
    expand_ref, out_ref, store_sem,
):
    loads = [
        pltpu.make_async_copy(source, target, load_sem.at[number])
        for number, (source, target) in enumerate(
            (
                (compress_hbm, compress_ref),
                (transfer_hbm, transfer_ref),
                (leaf_hbm.at[:, 0, :], leaf_ref),
                (parents_hbm, parents_ref),
                (table_hbm, table_ref),
                (spread_hbm, spread_ref),
                (expand_hbm, expand_ref),
            )
        )
    ]
    for load in loads:
        load.start()
    here = lax.axis_index("horiz")
    tile_x = here // grid_rows
    tile_y = here % grid_rows

    def present(dx, dy):
        x, y = tile_x + dx, tile_y + dy
        return (x >= 0) & (x < GRID_X) & (y >= 0) & (y < grid_rows)

    barrier = pltpu.get_barrier_semaphore()
    for dx, dy in DIRECTIONS:
        @pl.when(present(dx, dy))
        def _(dx=dx, dy=dy):
            pl.semaphore_signal(
                barrier, inc=1, device_id={"horiz": here + dx * grid_rows + dy},
                device_id_type=pl.DeviceIdType.MESH,
            )

    loads[0].wait()
    loads[1].wait()
    compress = compress_ref[...]
    both = jnp.dot(compress, transfer_ref[...], precision=HIGHEST, preferred_element_type=F32)
    loads[2].wait()
    fine, coarse = [], None
    for child in range(8):
        high, low = split(leaf_ref[:, child * BOXES : (child + 1) * BOXES])
        onto = jnp.concatenate([compress, both[:, child * 64 : (child + 1) * 64]], axis=0)
        onto_high, onto_low = split(onto)
        charged = jnp.dot(
            jnp.concatenate([onto_high, onto_low, onto_high], axis=1),
            jnp.concatenate([high, high, low], axis=0),
            preferred_element_type=F32,
        )
        fine.append(charged[:32])
        coarse = charged[32:] if coarse is None else coarse + charged[32:]
    fine_ref[...] = jnp.concatenate(fine, axis=0).T
    loads[3].wait()
    grouped = select_dot(coarse, parents_ref[...], NT)
    coarse_ref[...] = jnp.concatenate(
        [grouped[:, c * COARSE_ROWS : (c + 1) * COARSE_ROWS] for c in range(8)], axis=0
    ).T

    def pick(step, extent):
        return range(extent) if step == 0 else ([extent - 1] if step > 0 else [0])

    lengths = []
    for number, (dx, dy) in enumerate(DIRECTIONS):
        at = 0
        for x in pick(dx, PX):
            for y in pick(dy, PY):
                start = (x * PY + y) * PZ
                rim[number, at : at + PZ, :] = fine_ref[start : start + PZ, :]
                at += PZ
        for x in pick(dx, PX // 2):
            for y in pick(dy, PY // 2):
                start = (x * (PY // 2) + y) * COARSE_Z
                rim[number, at : at + COARSE_Z, :] = coarse_ref[start : start + COARSE_Z, :]
                at += COARSE_Z
        lengths.append(at)

    peers = sum(jnp.where(present(dx, dy), 1, 0) for dx, dy in DIRECTIONS)
    pl.semaphore_wait(barrier, peers)

    def copy_of(number):
        dx, dy = DIRECTIONS[number]
        return pltpu.make_async_remote_copy(
            src_ref=rim.at[number, pl.ds(0, lengths[number])],
            dst_ref=halo_ref.at[number, pl.ds(0, lengths[number])],
            send_sem=send_sem.at[number],
            recv_sem=recv_sem.at[number],
            device_id={"horiz": here + dx * grid_rows + dy},
            device_id_type=pl.DeviceIdType.MESH,
        )

    for number, (dx, dy) in enumerate(DIRECTIONS):
        @pl.when(present(dx, dy))
        def _(number=number):
            copy_of(number).start()

    for number, (dx, dy) in enumerate(DIRECTIONS):
        @pl.when(jnp.logical_not(present(-dx, -dy)))
        def _(number=number):
            halo_ref[number] = jnp.zeros(halo_ref.shape[1:], F32)

    loads[4].wait()
    loads[5].wait()
    build_weights(table_ref, spread_ref, high_ref, low_ref, cube, lanes_a, lanes_b)

    zero_rows = jnp.zeros((8, 256), F32)

    def place(x, y, rows):
        wide[x, y, 0:8, :] = zero_rows
        wide[x, y, 8 : 8 + PZ, :] = rows
        wide[x, y, 8 + PZ : 16 + PZ, :] = zero_rows

    def place_coarse(x, y, rows):
        wide_coarse[x, y, 0:8, :] = zero_rows
        wide_coarse[x, y, 8 : 8 + COARSE_Z, :] = rows
        wide_coarse[x, y, 8 + COARSE_Z : 16 + COARSE_Z, :] = zero_rows

    for x in range(PX):
        for y in range(PY):
            start = (x * PY + y) * PZ
            place(x + 1, y + 1, fine_ref[start : start + PZ, :])
    for x in range(PX // 2):
        for y in range(PY // 2):
            start = (x * (PY // 2) + y) * COARSE_Z
            place_coarse(x + 1, y + 1, coarse_ref[start : start + COARSE_Z, :])

    span = PY * PZ

    def windows(sy, columns):
        for sz in range(3):
            lanes = slice(sz * 256, (sz + 1) * 256)
            for x in columns:
                rows = jnp.concatenate(
                    [wide[x, sy + y, 7 + sz : 7 + sz + PZ, :] for y in range(PY)], axis=0
                )
                high, low = split(rows)
                wins_high[sy, x * span : (x + 1) * span, lanes] = high
                wins_low[sy, x * span : (x + 1) * span, lanes] = low

    def coarse_window(sx, sy, sz):
        return split(
            jnp.concatenate(
                [
                    wide_coarse[sx + x, sy + y, 7 + sz : 7 + sz + COARSE_Z, :]
                    for x in range(PX // 2)
                    for y in range(PY // 2)
                ],
                axis=0,
            )
        )

    def weight(ref, sx, sy, sz):
        rows = []
        for target in range(8):
            tx, ty, tz = target >> 2, target >> 1 & 1, target & 1
            at_y = (2 * sy + 1 - ty) * 32
            first = (2 * sz + 1 - tz) * 7 + 2 * sx + 1 - tx
            rows.append(
                jnp.concatenate(
                    [ref[first, at_y : at_y + 32, :], ref[first + 1, at_y : at_y + 32, :]], axis=1
                )
            )
        return jnp.concatenate(rows, axis=0)

    def apply(sx, sy):
        depths = (0, 2) if sx == 1 and sy == 1 else (0, 1, 2)
        rows = slice(sx * span, (sx + PX) * span)
        high, low, by_high, by_low = [], [], [], []
        for sz in depths:
            lanes = slice(sz * 256, (sz + 1) * 256)
            coarse_high, coarse_low = coarse_window(sx, sy, sz)
            high.append(jnp.concatenate([wins_high[sy, rows, lanes], coarse_high], axis=0))
            low.append(jnp.concatenate([wins_low[sy, rows, lanes], coarse_low], axis=0))
            by_high.append(weight(high_ref, sx, sy, sz))
            by_low.append(weight(low_ref, sx, sy, sz))
        product = lax.dot_general(
            jnp.concatenate(high + low + high, axis=1),
            jnp.concatenate(by_high + by_high + by_low, axis=1),
            NT,
            preferred_element_type=F32,
        )
        if sx == 1 and sy == 1:
            total[...] = product
        else:
            total[...] += product

    windows(1, range(1, PX + 1))
    apply(1, 1)

    for number, (dx, dy) in enumerate(DIRECTIONS):
        @pl.when(present(dx, dy))
        def _(number=number):
            copy_of(number).wait_send()

        @pl.when(present(-dx, -dy))
        def _(number=number):
            copy_of(number).wait_recv()

    def rim_places(step, extent):
        return range(1, extent + 1) if step == 0 else ([0] if step > 0 else [extent + 1])

    for number, (dx, dy) in enumerate(DIRECTIONS):
        at = 0
        for x in rim_places(dx, PX):
            for y in rim_places(dy, PY):
                place(x, y, halo_ref[number, at : at + PZ, :])
                at += PZ
        for x in rim_places(dx, PX // 2):
            for y in rim_places(dy, PY // 2):
                place_coarse(x, y, halo_ref[number, at : at + COARSE_Z, :])
                at += COARSE_Z

    windows(1, (0, PX + 1))
    apply(0, 1)
    apply(2, 1)
    for sy in (0, 2):
        windows(sy, range(PX + 2))
        for sx in range(3):
            apply(sx, sy)

    loads[6].wait()
    expand = expand_ref[...].T
    pushes = lax.dot_general(
        transfer_ref[...], expand, (((0,), (0,)), ((), ())), precision=HIGHEST,
        preferred_element_type=F32,
    )
    expand_high, expand_low = split(jnp.concatenate([expand] * 8, axis=1))
    push_high, push_low = split(pushes)
    child_of = lax.broadcasted_iota(jnp.int32, (64, 256), 1) // 32
    nothing = jnp.zeros((64, 256), BF16)
    spread_high = jnp.concatenate([jnp.where(child_of == c, expand_high, nothing) for c in range(8)])
    spread_low = jnp.concatenate([jnp.where(child_of == c, expand_low, nothing) for c in range(8)])

    across = (0.5 * total[BOXES:, :]).T
    across = jnp.concatenate([across[c * 32 : (c + 1) * 32] for c in range(8)], axis=1)
    coarse_field = select_dot(across, parents_ref[...], (((1,), (0,)), ((), ())))
    coarse_high, coarse_low = split(coarse_field)
    field_high, field_low = split(total[:BOXES, :])
    local = lax.dot_general(
        jnp.concatenate([spread_high, spread_low, spread_high], axis=1),
        jnp.concatenate([field_high, field_high, field_low], axis=1),
        NT,
        preferred_element_type=F32,
    ) + jnp.dot(
        jnp.concatenate([push_high, push_low, push_high], axis=1),
        jnp.concatenate([coarse_high, coarse_high, coarse_low], axis=0),
        preferred_element_type=F32,
    )
    stores = []
    for c in range(8):
        out_ref[:, c * BOXES : (c + 1) * BOXES] = local[c * 64 : (c + 1) * 64]
        stores.append(
            pltpu.make_async_copy(
                out_ref.at[:, pl.ds(c * BOXES, BOXES)],
                out_hbm.at[:, 0, pl.ds(c * BOXES, BOXES)],
                store_sem.at[c],
            )
        )
        stores[c].start()
    for store in stores:
        store.wait()


LIMIT = 58 * 1024 * 1024
HBM = pl.BlockSpec(memory_space=pltpu.HBM)


def shards(leaf_nodes, compress, expand, transfer, m2l_table):
    node_count = leaf_nodes.shape[0]
    grid_rows = lax.axis_size("horiz") // GRID_X
    parents = jnp.asarray(parent_selection())
    spread = jnp.asarray(table_selection())
    return pl.pallas_call(
        functools.partial(far_kernel, grid_rows),
        out_shape=jax.ShapeDtypeStruct(leaf_nodes.shape, F32),
        in_specs=[HBM] * 7,
        out_specs=HBM,
        scratch_shapes=[
            pltpu.VMEM((BOXES, 256), F32),
            pltpu.VMEM((COARSE_ROWS, 256), F32),
            pltpu.VMEM((8, RIM_ROWS, 256), F32),
            pltpu.VMEM((42, 192, 128), BF16),
            pltpu.VMEM((42, 192, 128), BF16),
            pltpu.VMEM((node_count, 8 * BOXES), F32),
            pltpu.VMEM(compress.shape, F32),
            pltpu.VMEM(transfer.shape, F32),
            pltpu.VMEM(parents.shape, BF16),
            pltpu.VMEM(m2l_table.shape, F32),
            pltpu.VMEM(spread.shape, BF16),
            pltpu.VMEM((8 * 56, 1024), F32),
            pltpu.VMEM((56 * 32, 128), F32),
            pltpu.VMEM((56 * 32, 128), F32),
            pltpu.VMEM((8, RIM_ROWS, 256), F32),
            pltpu.SemaphoreType.DMA((7,)),
            pltpu.SemaphoreType.DMA((8,)),
            pltpu.SemaphoreType.DMA((8,)),
            pltpu.VMEM((PX + 2, PY + 2, PZ + 16, 256), F32),
            pltpu.VMEM((PX // 2 + 2, PY // 2 + 2, COARSE_Z + 16, 256), F32),
            pltpu.VMEM((3, (PX + 2) * PY * PZ, 768), BF16),
            pltpu.VMEM((3, (PX + 2) * PY * PZ, 768), BF16),
            pltpu.VMEM((BOXES + COARSE_ROWS, 256), F32),
            pltpu.VMEM(expand.shape[::-1], F32),
            pltpu.VMEM((node_count, 8 * BOXES), F32),
            pltpu.SemaphoreType.DMA((8,)),
        ],
        compiler_params=pltpu.CompilerParams(
            collective_id=0, has_side_effects=True, vmem_limit_bytes=LIMIT
        ),
        name="far",
    )(leaf_nodes, compress, transfer, parents, m2l_table, spread, expand.T)


def solution(mesh):
    return jax.shard_map(
        shards,
        mesh=mesh,
        in_specs=(P("groups", "horiz", None), P(), P(), P(), P()),
        out_specs=P("groups", "horiz", None),
        check_vma=False,
    )
```

```python
import functools

import jax
import jax.numpy as jnp
import ml_dtypes
import numpy as np
from jax import lax
from jax.experimental import pallas as pl
from jax.experimental.pallas import tpu as pltpu
from jax.sharding import PartitionSpec as P

GRID_X = 8
PX = 4
PY = 4
PZ = 24
BOXES = PX * PY * PZ
COARSE_Z = 16
COARSE_ROWS = (PX // 2) * (PY // 2) * COARSE_Z
HIGHEST = lax.Precision.HIGHEST
BF16 = jnp.bfloat16
F32 = jnp.float32
DIRECTIONS = [(0, -1), (0, 1), (-1, 0), (1, 0), (-1, -1), (-1, 1), (1, -1), (1, 1)]
RIM_ROWS = PX * PZ + (PX // 2) * COARSE_Z
NT = (((1,), (1,)), ((), ()))


def table_selection():
    select = np.zeros((8 * 56, 316), np.float32)
    row = 0
    for dx in range(7):
        for dy in range(7):
            for dz in range(7):
                if max(abs(dx - 3), abs(dy - 3), abs(dz - 3)) >= 2:
                    select[dz * 56 + dx * 7 + dy, row] = 1.0
                    row += 1
    return select.astype(ml_dtypes.bfloat16)


def parent_selection():
    select = np.zeros((8 * COARSE_ROWS, BOXES), np.float32)
    for bx in range(PX):
        for by in range(PY):
            for bz in range(PZ):
                child = 4 * (bx % 2) + 2 * (by % 2) + bz % 2
                parent = ((bx // 2) * (PY // 2) + by // 2) * COARSE_Z + bz // 2
                select[child * COARSE_ROWS + parent, (bx * PY + by) * PZ + bz] = 1.0
    return select.astype(ml_dtypes.bfloat16)


def split(value):
    high = value.astype(BF16)
    return high, (value - high.astype(F32)).astype(BF16)


def select_dot(value, select, dims):
    high, low = split(value)
    return lax.dot_general(high, select, dims, preferred_element_type=F32) + lax.dot_general(
        low, select, dims, preferred_element_type=F32
    )


def build_weights(table_ref, select_ref, high_ref, low_ref, cube, lanes_a, lanes_b):
    table_high, table_low = split(table_ref[...])
    select = select_ref[...]
    cube[...] = jnp.dot(select, table_high, preferred_element_type=F32) + jnp.dot(
        select, table_low, preferred_element_type=F32
    )
    slot = lax.broadcasted_iota(jnp.int32, (56, 128), 1) // 32
    for half, out in enumerate((lanes_a, lanes_b)):
        for tile in range(8):
            parts = [
                cube[(4 * half + k) * 56 : (4 * half + k + 1) * 56, tile * 128 : (tile + 1) * 128]
                for k in range(4)
            ]
            for inner in range(4):
                merged = None
                for k in range(4):
                    by = (k - inner) % 4 * 32
                    moved = pltpu.roll(parts[k], by, 1) if by else parts[k]
                    merged = moved if merged is None else jnp.where(slot == k, moved, merged)
                out[pl.ds(tile * 4 + inner, 56, stride=32), :] = merged
    low_half = lax.broadcasted_iota(jnp.int32, (192, 128), 1) < 64
    lane = lax.broadcasted_iota(jnp.int32, (224, 128), 1)
    for dx in range(7):
        even0 = lanes_a[dx * 224 : (dx + 1) * 224, :]
        even1 = lanes_b[dx * 224 : (dx + 1) * 224, :]
        turned0 = pltpu.roll(even0, 96, 1)
        turned1 = pltpu.roll(even1, 96, 1)
        odd0 = jnp.where(lane < 96, turned0, turned1)
        odd1 = turned1
        for w, (source, straight) in enumerate(
            ((even0, True), (odd0, True), (even0, False), (odd0, False), (even1, True), (odd1, True))
        ):
            other = pltpu.roll(source, 64, 1)
            first, second = (source, other) if straight else (other, source)
            high, low = split(jnp.where(low_half, first[:192], second[32:]))
            high_ref[w * 7 + dx] = high
            low_ref[w * 7 + dx] = low


def far_kernel(
    grid_rows, leaf_hbm, compress_hbm, transfer_hbm, parents_hbm, table_hbm, spread_hbm,
    total_hbm, fine_ref, coarse_ref, halo_ref, high_ref, low_ref,
    leaf_ref, compress_ref, transfer_ref, parents_ref, table_ref, spread_ref,
    cube, lanes_a, lanes_b, rim, load_sem, send_sem, recv_sem,
    wide, wide_coarse, wins_high, wins_low, total,
    store_sem,
):
    loads = [
        pltpu.make_async_copy(source, target, load_sem.at[number])
        for number, (source, target) in enumerate(
            (
                (compress_hbm, compress_ref),
                (transfer_hbm, transfer_ref),
                (leaf_hbm.at[:, 0, :], leaf_ref),
                (parents_hbm, parents_ref),
                (table_hbm, table_ref),
                (spread_hbm, spread_ref),
            )
        )
    ]
    for load in loads:
        load.start()
    here = lax.axis_index("horiz")
    tile_x = here // grid_rows
    tile_y = here % grid_rows

    def present(dx, dy):
        x, y = tile_x + dx, tile_y + dy
        return (x >= 0) & (x < GRID_X) & (y >= 0) & (y < grid_rows)

    barrier = pltpu.get_barrier_semaphore()
    for dx, dy in DIRECTIONS:
        @pl.when(present(dx, dy))
        def _(dx=dx, dy=dy):
            pl.semaphore_signal(
                barrier, inc=1, device_id={"horiz": here + dx * grid_rows + dy},
                device_id_type=pl.DeviceIdType.MESH,
            )

    loads[0].wait()
    loads[1].wait()
    compress = compress_ref[...]
    both = jnp.dot(compress, transfer_ref[...], precision=HIGHEST, preferred_element_type=F32)
    loads[2].wait()
    fine, coarse = [], None
    for child in range(8):
        high, low = split(leaf_ref[:, child * BOXES : (child + 1) * BOXES])
        onto = jnp.concatenate([compress, both[:, child * 64 : (child + 1) * 64]], axis=0)
        onto_high, onto_low = split(onto)
        charged = jnp.dot(
            jnp.concatenate([onto_high, onto_low, onto_high], axis=1),
            jnp.concatenate([high, high, low], axis=0),
            preferred_element_type=F32,
        )
        fine.append(charged[:32])
        coarse = charged[32:] if coarse is None else coarse + charged[32:]
    fine_ref[...] = jnp.concatenate(fine, axis=0).T
    loads[3].wait()
    grouped = select_dot(coarse, parents_ref[...], NT)
    coarse_ref[...] = jnp.concatenate(
        [grouped[:, c * COARSE_ROWS : (c + 1) * COARSE_ROWS] for c in range(8)], axis=0
    ).T

    def pick(step, extent):
        return range(extent) if step == 0 else ([extent - 1] if step > 0 else [0])

    lengths = []
    for number, (dx, dy) in enumerate(DIRECTIONS):
        at = 0
        for x in pick(dx, PX):
            for y in pick(dy, PY):
                start = (x * PY + y) * PZ
                rim[number, at : at + PZ, :] = fine_ref[start : start + PZ, :]
                at += PZ
        for x in pick(dx, PX // 2):
            for y in pick(dy, PY // 2):
                start = (x * (PY // 2) + y) * COARSE_Z
                rim[number, at : at + COARSE_Z, :] = coarse_ref[start : start + COARSE_Z, :]
                at += COARSE_Z
        lengths.append(at)

    peers = sum(jnp.where(present(dx, dy), 1, 0) for dx, dy in DIRECTIONS)
    pl.semaphore_wait(barrier, peers)

    def copy_of(number):
        dx, dy = DIRECTIONS[number]
        return pltpu.make_async_remote_copy(
            src_ref=rim.at[number, pl.ds(0, lengths[number])],
            dst_ref=halo_ref.at[number, pl.ds(0, lengths[number])],
            send_sem=send_sem.at[number],
            recv_sem=recv_sem.at[number],
            device_id={"horiz": here + dx * grid_rows + dy},
            device_id_type=pl.DeviceIdType.MESH,
        )

    for number, (dx, dy) in enumerate(DIRECTIONS):
        @pl.when(present(dx, dy))
        def _(number=number):
            copy_of(number).start()

    for number, (dx, dy) in enumerate(DIRECTIONS):
        @pl.when(jnp.logical_not(present(-dx, -dy)))
        def _(number=number):
            halo_ref[number] = jnp.zeros(halo_ref.shape[1:], F32)

    loads[4].wait()
    loads[5].wait()
    build_weights(table_ref, spread_ref, high_ref, low_ref, cube, lanes_a, lanes_b)

    zero_rows = jnp.zeros((8, 256), F32)

    def place(x, y, rows):
        wide[x, y, 0:8, :] = zero_rows
        wide[x, y, 8 : 8 + PZ, :] = rows
        wide[x, y, 8 + PZ : 16 + PZ, :] = zero_rows

    def place_coarse(x, y, rows):
        wide_coarse[x, y, 0:8, :] = zero_rows
        wide_coarse[x, y, 8 : 8 + COARSE_Z, :] = rows
        wide_coarse[x, y, 8 + COARSE_Z : 16 + COARSE_Z, :] = zero_rows

    for x in range(PX):
        for y in range(PY):
            start = (x * PY + y) * PZ
            place(x + 1, y + 1, fine_ref[start : start + PZ, :])
    for x in range(PX // 2):
        for y in range(PY // 2):
            start = (x * (PY // 2) + y) * COARSE_Z
            place_coarse(x + 1, y + 1, coarse_ref[start : start + COARSE_Z, :])

    span = PY * PZ

    def windows(sy, columns):
        for sz in range(3):
            lanes = slice(sz * 256, (sz + 1) * 256)
            for x in columns:
                rows = jnp.concatenate(
                    [wide[x, sy + y, 7 + sz : 7 + sz + PZ, :] for y in range(PY)], axis=0
                )
                high, low = split(rows)
                wins_high[sy, x * span : (x + 1) * span, lanes] = high
                wins_low[sy, x * span : (x + 1) * span, lanes] = low

    def coarse_window(sx, sy, sz):
        return split(
            jnp.concatenate(
                [
                    wide_coarse[sx + x, sy + y, 7 + sz : 7 + sz + COARSE_Z, :]
                    for x in range(PX // 2)
                    for y in range(PY // 2)
                ],
                axis=0,
            )
        )

    def weight(ref, sx, sy, sz):
        rows = []
        for target in range(8):
            tx, ty, tz = target >> 2, target >> 1 & 1, target & 1
            at_y = (2 * sy + 1 - ty) * 32
            first = (2 * sz + 1 - tz) * 7 + 2 * sx + 1 - tx
            rows.append(
                jnp.concatenate(
                    [ref[first, at_y : at_y + 32, :], ref[first + 1, at_y : at_y + 32, :]], axis=1
                )
            )
        return jnp.concatenate(rows, axis=0)

    def apply(sx, sy):
        depths = (0, 2) if sx == 1 and sy == 1 else (0, 1, 2)
        rows = slice(sx * span, (sx + PX) * span)
        high, low, by_high, by_low = [], [], [], []
        for sz in depths:
            lanes = slice(sz * 256, (sz + 1) * 256)
            coarse_high, coarse_low = coarse_window(sx, sy, sz)
            high.append(jnp.concatenate([wins_high[sy, rows, lanes], coarse_high], axis=0))
            low.append(jnp.concatenate([wins_low[sy, rows, lanes], coarse_low], axis=0))
            by_high.append(weight(high_ref, sx, sy, sz))
            by_low.append(weight(low_ref, sx, sy, sz))
        product = lax.dot_general(
            jnp.concatenate(high + low + high, axis=1),
            jnp.concatenate(by_high + by_high + by_low, axis=1),
            NT,
            preferred_element_type=F32,
        )
        if sx == 1 and sy == 1:
            total[...] = product
        else:
            total[...] += product

    windows(1, range(1, PX + 1))
    apply(1, 1)

    for number, (dx, dy) in enumerate(DIRECTIONS):
        @pl.when(present(dx, dy))
        def _(number=number):
            copy_of(number).wait_send()

        @pl.when(present(-dx, -dy))
        def _(number=number):
            copy_of(number).wait_recv()

    def rim_places(step, extent):
        return range(1, extent + 1) if step == 0 else ([0] if step > 0 else [extent + 1])

    for number, (dx, dy) in enumerate(DIRECTIONS):
        at = 0
        for x in rim_places(dx, PX):
            for y in rim_places(dy, PY):
                place(x, y, halo_ref[number, at : at + PZ, :])
                at += PZ
        for x in rim_places(dx, PX // 2):
            for y in rim_places(dy, PY // 2):
                place_coarse(x, y, halo_ref[number, at : at + COARSE_Z, :])
                at += COARSE_Z

    windows(1, (0, PX + 1))
    apply(0, 1)
    apply(2, 1)
    for sy in (0, 2):
        windows(sy, range(PX + 2))
        for sx in range(3):
            apply(sx, sy)

    store = pltpu.make_async_copy(total, total_hbm, store_sem.at[0])
    store.start()
    store.wait()


def expansions_kernel(
    expand_hbm, transfer_hbm, total_hbm, parents_hbm, out_hbm,
    expand_ref, transfer_ref, total, parents_ref, out_ref, load_sem, store_sem,
):
    loads = [
        pltpu.make_async_copy(source, target, load_sem.at[number])
        for number, (source, target) in enumerate(
            (
                (expand_hbm, expand_ref),
                (transfer_hbm, transfer_ref),
                (total_hbm, total),
                (parents_hbm, parents_ref),
            )
        )
    ]
    for load in loads:
        load.start()
    for load in loads[:2]:
        load.wait()
    expand = expand_ref[...].T
    pushes = lax.dot_general(
        transfer_ref[...], expand, (((0,), (0,)), ((), ())), precision=HIGHEST,
        preferred_element_type=F32,
    )
    expand_high, expand_low = split(jnp.concatenate([expand] * 8, axis=1))
    push_high, push_low = split(pushes)
    child_of = lax.broadcasted_iota(jnp.int32, (64, 256), 1) // 32
    nothing = jnp.zeros((64, 256), BF16)
    spread_high = jnp.concatenate([jnp.where(child_of == c, expand_high, nothing) for c in range(8)])
    spread_low = jnp.concatenate([jnp.where(child_of == c, expand_low, nothing) for c in range(8)])

    for load in loads[2:]:
        load.wait()
    across = (0.5 * total[BOXES:, :]).T
    across = jnp.concatenate([across[c * 32 : (c + 1) * 32] for c in range(8)], axis=1)
    coarse_field = select_dot(across, parents_ref[...], (((1,), (0,)), ((), ())))
    coarse_high, coarse_low = split(coarse_field)
    field_high, field_low = split(total[:BOXES, :])
    local = lax.dot_general(
        jnp.concatenate([spread_high, spread_low, spread_high], axis=1),
        jnp.concatenate([field_high, field_high, field_low], axis=1),
        NT,
        preferred_element_type=F32,
    ) + jnp.dot(
        jnp.concatenate([push_high, push_low, push_high], axis=1),
        jnp.concatenate([coarse_high, coarse_high, coarse_low], axis=0),
        preferred_element_type=F32,
    )
    stores = []
    for c in range(8):
        out_ref[:, c * BOXES : (c + 1) * BOXES] = local[c * 64 : (c + 1) * 64]
        stores.append(
            pltpu.make_async_copy(
                out_ref.at[:, pl.ds(c * BOXES, BOXES)],
                out_hbm.at[:, 0, pl.ds(c * BOXES, BOXES)],
                store_sem.at[c],
            )
        )
        stores[c].start()
    for store in stores:
        store.wait()


LIMIT = 58 * 1024 * 1024
HBM = pl.BlockSpec(memory_space=pltpu.HBM)


def shards(leaf_nodes, compress, expand, transfer, m2l_table):
    node_count = leaf_nodes.shape[0]
    grid_rows = lax.axis_size("horiz") // GRID_X
    parents = jnp.asarray(parent_selection())
    spread = jnp.asarray(table_selection())
    total = pl.pallas_call(
        functools.partial(far_kernel, grid_rows),
        out_shape=jax.ShapeDtypeStruct((BOXES + COARSE_ROWS, 256), F32),
        in_specs=[HBM] * 6,
        out_specs=HBM,
        scratch_shapes=[
            pltpu.VMEM((BOXES, 256), F32),
            pltpu.VMEM((COARSE_ROWS, 256), F32),
            pltpu.VMEM((8, RIM_ROWS, 256), F32),
            pltpu.VMEM((42, 192, 128), BF16),
            pltpu.VMEM((42, 192, 128), BF16),
            pltpu.VMEM((node_count, 8 * BOXES), F32),
            pltpu.VMEM(compress.shape, F32),
            pltpu.VMEM(transfer.shape, F32),
            pltpu.VMEM(parents.shape, BF16),
            pltpu.VMEM(m2l_table.shape, F32),
            pltpu.VMEM(spread.shape, BF16),
            pltpu.VMEM((8 * 56, 1024), F32),
            pltpu.VMEM((56 * 32, 128), F32),
            pltpu.VMEM((56 * 32, 128), F32),
            pltpu.VMEM((8, RIM_ROWS, 256), F32),
            pltpu.SemaphoreType.DMA((6,)),
            pltpu.SemaphoreType.DMA((8,)),
            pltpu.SemaphoreType.DMA((8,)),
            pltpu.VMEM((PX + 2, PY + 2, PZ + 16, 256), F32),
            pltpu.VMEM((PX // 2 + 2, PY // 2 + 2, COARSE_Z + 16, 256), F32),
            pltpu.VMEM((3, (PX + 2) * PY * PZ, 768), BF16),
            pltpu.VMEM((3, (PX + 2) * PY * PZ, 768), BF16),
            pltpu.VMEM((BOXES + COARSE_ROWS, 256), F32),
            pltpu.SemaphoreType.DMA((1,)),
        ],
        compiler_params=pltpu.CompilerParams(
            collective_id=0, has_side_effects=True, vmem_limit_bytes=LIMIT
        ),
        name="far",
    )(leaf_nodes, compress, transfer, parents, m2l_table, spread)
    return pl.pallas_call(
        expansions_kernel,
        out_shape=jax.ShapeDtypeStruct(leaf_nodes.shape, F32),
        in_specs=[HBM] * 4,
        out_specs=HBM,
        scratch_shapes=[
            pltpu.VMEM(expand.shape[::-1], F32),
            pltpu.VMEM(transfer.shape, F32),
            pltpu.VMEM((BOXES + COARSE_ROWS, 256), F32),
            pltpu.VMEM(parents.shape, BF16),
            pltpu.VMEM((node_count, 8 * BOXES), F32),
            pltpu.SemaphoreType.DMA((4,)),
            pltpu.SemaphoreType.DMA((8,)),
        ],
        compiler_params=pltpu.CompilerParams(vmem_limit_bytes=LIMIT),
        name="expansions",
    )(expand.T, transfer, total, parents)


def solution(mesh):
    return jax.shard_map(
        shards,
        mesh=mesh,
        in_specs=(P("groups", "horiz", None), P(), P(), P(), P()),
        out_specs=P("groups", "horiz", None),
        check_vma=False,
    )
```
